32 devices in a mesh: lon: 8 (over z, core), lat: 4 (over y, x).
Axes of the slice: x: 2, y: 2, z: 4, core: 2. Of those that a mesh axis runs over, the one named last changes fastest.
Arguments:
- state: float32 [16, 128, 2048], P(None, 'lat', 'lon'), may hold values from -6 to 6
- coef_lon: float32 [128, 2048], P('lat', 'lon'), may hold values from 0.2 to 0.24
- coef_lat: float32 [128, 2048], P('lat', 'lon'), may hold values from 0.2 to 0.24
- land_sea: int32 [128, 2048], P('lat', 'lon'), may hold values 0 or 1
- send_cols: int32 [4, 32768], P('lat', 'lon'), may hold values from 0 to 8191
- send_count: int32 [4, 64], P('lat', 'lon'), may hold values from 64 to 512, as said below
- obs_value: float32 [16, 4, 32768], P(None, 'lat', 'lon'), may hold values from -6 to 6
- obs_weight: float32 [16, 4, 32768], P(None, 'lat', 'lon'), may hold values from 0.25 to 4
Outputs:
- increment: float32 [16, 128, 2048], P(None, 'lat', 'lon')
The draws below stay inside these ranges and needn't reach their ends.
Inputs may be any that keep to these rules, and one draw needn't show every extreme that they name: `send_count`: at most 512 live slots go from one device to one peer; in every latitude band some receiving device gets 512 from every device of the band, which one drawn from the seed. `send_cols`: entries index a column of the sending device's own block, row-major over its 32 x 256 cells.
All inputs are finite; a program needn't handle non-finite values. No bound on the sum of `land_sea` on one device may be relied on, other than what follows from the above.
Results may differ from the reference program's by a relative error of at most 0.00002.
Values sent between devices are 32-bit elements; how exact they have to be, the bound alone decides.
A program may use at most 64 MiB of HBM per device.

```python
import math
import jax
import jax.numpy as jnp
from jax import lax

LEV = 16
CLAT = 32
CLON = 256
SLOTS_DEV = 4096
PASSES = 8
CAP = 512
NLAT = 128
NLON = 2048
N_LON = 8
N_LAT = 4


def draw_send_count(key, part):
    capacity = SLOTS_DEV // N_LON
    base_load = jax.random.randint(jax.random.fold_in(key, 11), (N_LAT, N_LON, N_LON), capacity // 8, 3 * capacity // 4 + 1)
    busiest = jax.random.randint(jax.random.fold_in(key, 12), (N_LAT, 1, 1), 0, N_LON)
    dest_index = jnp.arange(N_LON, dtype=jnp.int32)[None, None, :]
    loads = jnp.where(dest_index == busiest, capacity, base_load)
    return loads.reshape(N_LAT, N_LON * N_LON).astype(jnp.int32)


def with_ends(drawn, key, smallest, largest):
    longest = drawn.shape.index(max(drawn.shape))
    spots = []
    for shift in (0, 1):
        where = [jax.random.randint(jax.random.fold_in(key, axis), (), 0, length) for axis, length in enumerate(drawn.shape)]
        where[longest] = (where[longest] + shift) % drawn.shape[longest]
        spots.append(tuple(where))
    return drawn.at[spots[0]].set(smallest).at[spots[1]].set(largest)


def steps_of(stream_key, extent, shards, least, top_value):
    def one(dim, shards_of):
        steps = jax.random.uniform(jax.random.fold_in(jax.random.fold_in(stream_key, 6), dim), (shards_of,), jnp.float32, least / len(shards), top_value / len(shards))
        return jnp.repeat(jnp.exp(steps), extent[dim] // shards_of).reshape((-1,) + (1,) * (len(extent) - dim - 1))

    gain = one(*shards[0])
    for cut in shards[1:]:
        gain = gain * one(*cut)
    return gain


def noise(stream_key, shape, scale, bound, pieces=(), held_as=jnp.bfloat16):
    values = jax.random.normal(stream_key, shape, jnp.float32) * scale
    if len(pieces) > 0:
        values = steps_of(stream_key, shape, pieces, -0.22, 0.18) * values
    return jnp.clip(values, min=-bound, max=bound).astype(held_as)


def setup_inputs(seed: int = 0) -> dict:
    seeds = jax.random.split(jax.random.key(seed), 9)
    state = noise(seeds[0], (LEV, NLAT, NLON), 1.0, 6.0, ((1, 4), (2, 8)), jnp.float32)
    coef_lon = jnp.clip(0.2 + 0.03999999 * jax.random.uniform(seeds[1], (NLAT, NLON), jnp.float32) ** steps_of(seeds[1], (NLAT, NLON), ((0, 4), (1, 8)), -0.2, 0.2), 0.2, 0.24)
    coef_lat = jnp.clip(0.2 + 0.03999999 * jax.random.uniform(seeds[2], (NLAT, NLON), jnp.float32) ** steps_of(seeds[2], (NLAT, NLON), ((0, 4), (1, 8)), -0.2, 0.2), 0.2, 0.24)
    land_sea = with_ends((jax.random.randint(seeds[3], (NLAT, NLON), 0, 20) < 19).astype(jnp.int32), jax.random.fold_in(seeds[3], 1), 0, 1)
    send_cols = with_ends(jax.random.randint(seeds[4], (N_LAT, N_LON * SLOTS_DEV), 0, CLAT * CLON), jax.random.fold_in(seeds[4], 1), 0, (CLAT * CLON) - 1).astype(jnp.int32)
    send_count = draw_send_count(jax.random.fold_in(seeds[8], 71), 0)
    obs_value = noise(seeds[6], (LEV, N_LAT, N_LON * SLOTS_DEV), 1.0, 6.0, ((1, 4), (2, 8)), jnp.float32)
    obs_weight = jnp.clip(jnp.exp(math.log(4.0) - 2.7725887 * jax.random.uniform(seeds[7], (LEV, N_LAT, N_LON * SLOTS_DEV), jnp.float32) ** steps_of(seeds[7], (LEV, N_LAT, N_LON * SLOTS_DEV), ((1, 4), (2, 8)), -0.2, 0.2)), 0.25, 4.0)
    return dict(state=state, coef_lon=coef_lon, coef_lat=coef_lat, land_sea=land_sea, send_cols=send_cols, send_count=send_count, obs_value=obs_value, obs_weight=obs_weight)


def reference(state, coef_lon, coef_lat, land_sea, send_cols, send_count, obs_value, obs_weight):
    targets = send_cols.reshape(N_LAT, N_LON, SLOTS_DEV)
    band_index = jnp.arange(N_LAT, dtype=jnp.int32)[:, None, None]
    owner_index = jnp.arange(N_LON, dtype=jnp.int32)[None, :, None]
    glob_rows = band_index * CLAT + targets // CLON
    glob_cols = owner_index * CLON + targets % CLON
    flat_index = (glob_rows * NLON + glob_cols).reshape(-1).astype(jnp.int32)
    columns = state.reshape(LEV, NLAT * NLON)
    seen = jnp.take(columns, flat_index, axis=1).reshape(LEV, N_LAT, N_LON, N_LON, CAP)
    values = jnp.transpose(obs_value.reshape(LEV, N_LAT, N_LON, N_LON, CAP), (0, 1, 3, 2, 4))
    weights = jnp.transpose(obs_weight.reshape(LEV, N_LAT, N_LON, N_LON, CAP), (0, 1, 3, 2, 4))
    slot_index = jnp.arange(CAP, dtype=jnp.int32)
    counts = send_count.reshape(N_LAT, N_LON, N_LON)
    usable = jnp.where(slot_index[None, None, None, :] < counts[..., None], 1.0, 0.0).astype(jnp.float32)
    weighted = weights * (values - seen) * usable[None]
    gradient = jnp.zeros((LEV, NLAT * NLON), jnp.float32).at[:, flat_index].add(weighted.reshape(LEV, -1))
    sea = land_sea.astype(jnp.float32)
    gradient = gradient.reshape(LEV, NLAT, NLON) * sea[None]
    east_face = coef_lon * sea * jnp.roll(sea, -1, axis=1)
    zero_row = jnp.zeros((1, NLON), jnp.float32)
    north_face = coef_lat * sea * jnp.concatenate([sea[1:], zero_row], axis=0)

    def diffuse(layer_field):
        for step_number in range(PASSES):
            flux_east = east_face * (jnp.roll(layer_field, -1, axis=1) - layer_field)
            upper = jnp.concatenate([layer_field[1:], zero_row], axis=0)
            flux_north = north_face * (upper - layer_field)
            flux_west = jnp.roll(flux_east, 1, axis=1)
            flux_south = jnp.concatenate([zero_row, flux_north[:-1]], axis=0)
            layer_field = layer_field + flux_east - flux_west + flux_north - flux_south
        return layer_field

    return lax.map(diffuse, gradient)
```

```python
import functools

import jax
import jax.numpy as jnp
from jax import lax
from jax.experimental import pallas as pl
from jax.experimental.pallas import tpu as pltpu
from jax.sharding import PartitionSpec as P

PASSES = 8
MESH = pl.DeviceIdType.MESH
F32 = jnp.float32
BF16 = jnp.bfloat16


def pieces_of(x):
    first = x.astype(BF16)
    rest = x - first.astype(F32)
    second = rest.astype(BF16)
    third = (rest - second.astype(F32)).astype(BF16)
    return first, second, third


def kernel(
    n_lon, n_lat,
    state_ref, coef_lon_ref, coef_lat_ref, land_ref, cols_ref, count_ref, value_ref, weight_ref,
    out_ref,
    recv, seen, hot, spread, spread_bf, pieces, scattered, coefs, coef_out, coef_west, coef_east,
    east_b, north_b, field, edge_out, edge_west, edge_east,
    own_sem, send_sem, recv_sem, csend_sem, crecv_sem, gsend_sem, grecv_sem,
):
    levels, rows, cols = state_ref.shape
    halo = PASSES
    ext = rows + 2 * halo
    lanes = cols + 128
    cap = recv.shape[3]
    lon = lax.axis_index("lon")
    lat = lax.axis_index("lat")
    east, west = lax.rem(lon + 1, n_lon), lax.rem(lon + n_lon - 1, n_lon)
    north, south = lax.rem(lat + 1, n_lat), lax.rem(lat + n_lat - 1, n_lat)

    def at(lon_to, lat_to):
        return {"lon": lon_to, "lat": lat_to}

    around = [
        at(lon, north), at(lon, south), at(east, lat), at(west, lat),
        at(east, north), at(west, north), at(east, south), at(west, south),
    ]
    barrier = pltpu.get_barrier_semaphore()
    for step in range(1, n_lon):
        pl.semaphore_signal(
            barrier, inc=1, device_id=at(lax.rem(lon + step, n_lon), lat), device_id_type=MESH
        )
    for place in (0, 1, 4, 5, 6, 7):
        pl.semaphore_signal(barrier, inc=1, device_id=around[place], device_id_type=MESH)
    pl.semaphore_wait(barrier, n_lon - 1 + 6)

    sources = (value_ref, weight_ref)

    def profile_copy(which, step):
        peer = lax.rem(lon + step, n_lon)
        start = pl.multiple_of(peer * cap, 128)
        return pltpu.make_async_remote_copy(
            src_ref=sources[which].at[:, pl.ds(start, cap)],
            dst_ref=recv.at[which, step],
            send_sem=send_sem.at[which, step],
            recv_sem=recv_sem.at[which, step],
            device_id=at(peer, lat),
            device_id_type=MESH,
        )

    half = n_lon // 2
    order = []
    for off in range(half, 0, -1):
        order += [off] if 2 * off == n_lon else [off, n_lon - off]
    for step in order:
        for which in (0, 1):
            profile_copy(which, step).start()
    own = [
        pltpu.make_async_copy(
            sources[which].at[:, pl.ds(pl.multiple_of(lon * cap, 128), cap)],
            recv.at[which, 0],
            own_sem.at[which],
        )
        for which in (0, 1)
    ]
    for copy in own:
        copy.start()

    here = pl.ds(halo, rows)
    coefs[0, here, 0:cols] = land_ref[...].astype(F32)
    coefs[1, here, 0:cols] = coef_lon_ref[...]
    coefs[2, here, 0:cols] = coef_lat_ref[...]
    lane = lax.broadcasted_iota(jnp.int32, (rows, 128), 1)
    to_east = jnp.zeros((rows, 128), F32)
    to_west = jnp.zeros((rows, 128), F32)
    for a in range(3):
        low = coefs[a, here, 0:128]
        high = coefs[a, here, cols - 128:cols]
        mine = (lane >= 8 * a) & (lane < 8 * a + 8)
        to_east = jnp.where(mine, pltpu.roll(high, (8 * a + 8) % 128, axis=1), to_east)
        to_west = jnp.where(mine, low if a == 0 else pltpu.roll(low, 8 * a, axis=1), to_west)
    coef_out[0] = to_east
    coef_out[1] = to_west
    top, bottom = pl.ds(rows - halo, halo), pl.ds(0, halo)
    low_rim, high_rim = pl.ds(0, halo), pl.ds(halo + rows, halo)
    coef_moves = [
        (coefs.at[:, pl.ds(rows, halo), 0:cols], coefs.at[:, low_rim, 0:cols]),
        (coefs.at[:, pl.ds(halo, halo), 0:cols], coefs.at[:, high_rim, 0:cols]),
        (coef_out.at[0], coef_west.at[here]),
        (coef_out.at[1], coef_east.at[here]),
        (coef_out.at[0, top], coef_west.at[low_rim]),
        (coef_out.at[1, top], coef_east.at[low_rim]),
        (coef_out.at[0, bottom], coef_west.at[high_rim]),
        (coef_out.at[1, bottom], coef_east.at[high_rim]),
    ]
    coef_copies = [
        pltpu.make_async_remote_copy(
            src_ref=src, dst_ref=dst, send_sem=csend_sem.at[i], recv_sem=crecv_sem.at[i],
            device_id=around[i], device_id_type=MESH,
        )
        for i, (src, dst) in enumerate(coef_moves)
    ]
    for copy in coef_copies:
        copy.start()

    for r in range(rows):
        parts = pieces_of(state_ref[:, r, :])
        for i in range(3):
            pieces[i, levels * r:levels * (r + 1), :] = parts[i]

    def places(step):
        holder = lax.rem(lon + n_lon - step, n_lon)
        entry = cols_ref[:, pl.ds(pl.multiple_of(holder * cap, 128), cap)]
        return holder, entry // cols, entry % cols

    def gather_step(step, carry):
        _, row, col = places(step)
        which_col = lax.broadcasted_iota(jnp.int32, (cols, cap), 0)
        one_hot = jnp.where(which_col == col, 1.0, 0.0).astype(BF16)
        hot[step] = one_hot
        picked = jnp.dot(pieces[0], one_hot, preferred_element_type=F32)
        picked += jnp.dot(pieces[1], one_hot, preferred_element_type=F32)
        picked += jnp.dot(pieces[2], one_hot, preferred_element_type=F32)
        spread[...] = picked
        row_b = jnp.broadcast_to(row, (levels, cap))
        total = jnp.zeros((levels, cap), F32)
        for r in range(rows):
            total += jnp.where(row_b == r, spread[levels * r:levels * (r + 1), :], 0.0)
        seen[step] = total
        return carry

    lax.fori_loop(0, n_lon, gather_step, 0)

    for copy in coef_copies:
        copy.wait()
    lane_e = lax.broadcasted_iota(jnp.int32, (ext, 128), 1)
    from_west, from_east = coef_west[...], coef_east[...]
    for a in range(3):
        eastern = from_east if a == 0 else pltpu.roll(from_east, 128 - 8 * a, axis=1)
        western = pltpu.roll(from_west, 120 - 8 * a, axis=1)
        coefs[a, :, cols:lanes] = jnp.where(
            lane_e < 8, eastern, jnp.where(lane_e >= 120, western, 0.0)
        )
    row_place = lax.broadcasted_iota(jnp.int32, (ext, lanes), 0)
    first_out = jnp.where(lat == 0, halo, 0)
    last_out = jnp.where(lat == n_lat - 1, halo + rows, ext)
    inside = (row_place >= first_out) & (row_place < last_out)
    sea = jnp.where(inside, coefs[0], 0.0)
    coefs[0] = sea
    east_face = coefs[1] * sea * pltpu.roll(sea, lanes - 1, axis=1)
    north_face = coefs[2] * sea * pltpu.roll(sea, ext - 1, axis=0)
    for e in range(ext):
        east_b[e] = jnp.broadcast_to(east_face[e:e + 1, :], (8, lanes))
        north_b[e] = jnp.broadcast_to(north_face[e:e + 1, :], (8, lanes))

    scattered[...] = jnp.zeros_like(scattered)

    def scatter_step(step, carry):
        holder, row, _ = places(step)
        for which in (0, 1):

            @pl.when(step == 0)
            def _():
                own[which].wait()

            @pl.when(step != 0)
            def _():
                profile_copy(which, step).wait_recv()

        slot = lax.broadcasted_iota(jnp.int32, (levels, cap), 1)
        usable = jnp.where(slot < count_ref[0, holder], 1.0, 0.0)
        weighted = recv[1, step] * (recv[0, step] - seen[step]) * usable
        parts = pieces_of(weighted)
        row_b = jnp.broadcast_to(row, (levels, cap))
        for r in range(rows):
            mine = jnp.where(row_b == r, 1.0, 0.0).astype(BF16)
            for i in range(3):
                spread_bf[i, levels * r:levels * (r + 1), :] = mine * parts[i]
        one_hot = hot[step]
        dims = (((1,), (1,)), ((), ()))
        total = lax.dot_general(spread_bf[0], one_hot, dims, preferred_element_type=F32)
        total += lax.dot_general(spread_bf[1], one_hot, dims, preferred_element_type=F32)
        total += lax.dot_general(spread_bf[2], one_hot, dims, preferred_element_type=F32)
        scattered[...] += total
        return carry

    lax.fori_loop(0, n_lon, scatter_step, 0)

    for r in range(rows):
        sea_r = jnp.broadcast_to(coefs[0, halo + r:halo + r + 1, 0:cols], (levels, cols))
        field[0, halo + r, :, 0:cols] = scattered[levels * r:levels * (r + 1), :] * sea_r
    group = 128 // halo
    blocks = rows // group
    lane_g = lax.broadcasted_iota(jnp.int32, (levels, 128), 1)
    for j in range(blocks):
        to_east = jnp.zeros((levels, 128), F32)
        to_west = jnp.zeros((levels, 128), F32)
        for k in range(group):
            low = field[0, halo + j * group + k, :, 0:128]
            high = field[0, halo + j * group + k, :, cols - 128:cols]
            mine = (lane_g >= 8 * k) & (lane_g < 8 * k + 8)
            to_east = jnp.where(mine, pltpu.roll(high, (8 * k + 8) % 128, axis=1) if k < group - 1 else high, to_east)
            to_west = jnp.where(mine, low if k == 0 else pltpu.roll(low, 8 * k, axis=1), to_west)
        edge_out[0, j] = to_east
        edge_out[1, j] = to_west
    middle = pl.ds(1, blocks)
    field_moves = [
        (field.at[0, pl.ds(rows, halo), :, 0:cols], field.at[0, low_rim, :, 0:cols]),
        (field.at[0, pl.ds(halo, halo), :, 0:cols], field.at[0, high_rim, :, 0:cols]),
        (edge_out.at[0], edge_west.at[middle]),
        (edge_out.at[1], edge_east.at[middle]),
        (edge_out.at[0, blocks - 1], edge_west.at[0]),
        (edge_out.at[1, blocks - 1], edge_east.at[0]),
        (edge_out.at[0, 0], edge_west.at[blocks + 1]),
        (edge_out.at[1, 0], edge_east.at[blocks + 1]),
    ]
    field_copies = [
        pltpu.make_async_remote_copy(
            src_ref=src, dst_ref=dst, send_sem=gsend_sem.at[i], recv_sem=grecv_sem.at[i],
            device_id=around[i], device_id_type=MESH,
        )
        for i, (src, dst) in enumerate(field_moves)
    ]
    for i in (2, 3, 0, 1, 4, 5, 6, 7):
        field_copies[i].start()

    def unpack(first, last):
        for e in range(first, last):
            j, k = (e + halo) // group, (e + halo) % group
            eastern = edge_east[j]
            if k > 0:
                eastern = pltpu.roll(eastern, 128 - 8 * k, axis=1)
            western = edge_west[j]
            if k < group - 1:
                western = pltpu.roll(western, 120 - 8 * k, axis=1)
            field[0, e, :, cols:lanes] = jnp.where(
                lane_g < 8, eastern, jnp.where(lane_g >= 120, western, 0.0)
            )

    def twice(face):
        return jnp.concatenate([face] * (levels // 8), axis=0)

    def advance(t, first, last):
        before = field.at[t - 1]
        start = before[first]
        flux_in = twice(north_b[first - 1]) * (start - before[first - 1])

        def row_step(e, carry):
            g, flux_south = carry
            g_north = before[e + 1]
            flux_north = twice(north_b[e]) * (g_north - g)
            flux_east = twice(east_b[e]) * (pltpu.roll(g, lanes - 1, axis=1) - g)
            new = g + flux_east - pltpu.roll(flux_east, 1, axis=1) + flux_north - flux_south
            if t == PASSES:
                out_ref[e - halo] = new[:, 0:cols]
            else:
                field[t, e] = new
            return g_north, flux_north

        lax.fori_loop(first, last, row_step, (start, flux_in), unroll=2)

    field_copies[2].wait_recv()
    field_copies[3].wait_recv()
    unpack(halo, halo + rows)
    for t in range(1, PASSES + 1):
        advance(t, halo + t, halo + rows - t)
    for i in (0, 1, 4, 5, 6, 7):
        field_copies[i].wait_recv()
    unpack(0, halo)
    unpack(halo + rows, ext)
    for t in range(1, PASSES + 1):
        advance(t, t, halo + t)
        advance(t, halo + rows - t, ext - t)

    for step in order:
        for which in (0, 1):
            profile_copy(which, step).wait_send()
    for copy in field_copies:
        copy.wait_send()


def body(state, coef_lon, coef_lat, land_sea, send_cols, send_count, obs_value, obs_weight):
    levels, rows, cols = state.shape
    n_lon = lax.axis_size("lon")
    n_lat = lax.axis_size("lat")
    slots = send_cols.shape[1]
    cap = slots // n_lon
    ext, lanes = rows + 2 * PASSES, cols + 128
    blocks = rows * PASSES // 128
    vmem = pl.BlockSpec(memory_space=pltpu.VMEM)
    anywhere = pl.BlockSpec(memory_space=pl.ANY)
    dma = pltpu.SemaphoreType.DMA
    out = pl.pallas_call(
        functools.partial(kernel, n_lon, n_lat),
        out_shape=jax.ShapeDtypeStruct((rows, levels, cols), F32),
        in_specs=[vmem] * 5 + [pl.BlockSpec(memory_space=pltpu.SMEM)] + [anywhere] * 2,
        out_specs=vmem,
        scratch_shapes=[
            pltpu.VMEM((2, n_lon, levels, cap), F32),
            pltpu.VMEM((n_lon, levels, cap), F32),
            pltpu.VMEM((n_lon, cols, cap), BF16),
            pltpu.VMEM((rows * levels, cap), F32),
            pltpu.VMEM((3, rows * levels, cap), BF16),
            pltpu.VMEM((3, rows * levels, cols), BF16),
            pltpu.VMEM((rows * levels, cols), F32),
            pltpu.VMEM((3, ext, lanes), F32),
            pltpu.VMEM((2, rows, 128), F32),
            pltpu.VMEM((ext, 128), F32),
            pltpu.VMEM((ext, 128), F32),
            pltpu.VMEM((ext, 8, lanes), F32),
            pltpu.VMEM((ext, 8, lanes), F32),
            pltpu.VMEM((PASSES, ext, levels, lanes), F32),
            pltpu.VMEM((2, blocks, levels, 128), F32),
            pltpu.VMEM((blocks + 2, levels, 128), F32),
            pltpu.VMEM((blocks + 2, levels, 128), F32),
            dma((2,)),
            dma((2, n_lon)),
            dma((2, n_lon)),
            dma((8,)),
            dma((8,)),
            dma((8,)),
            dma((8,)),
        ],
        compiler_params=pltpu.CompilerParams(
            collective_id=0, has_side_effects=True, vmem_limit_bytes=48 * 2**20
        ),
        name="analysis",
    )(
        state, coef_lon, coef_lat, land_sea, send_cols, send_count,
        obs_value.reshape(levels, slots), obs_weight.reshape(levels, slots),
    )
    return jnp.transpose(out, (1, 0, 2))


def solution(mesh):
    placed = (
        P(None, "lat", "lon"),
        P("lat", "lon"),
        P("lat", "lon"),
        P("lat", "lon"),
        P("lat", "lon"),
        P("lat", "lon"),
        P(None, "lat", "lon"),
        P(None, "lat", "lon"),
    )
    return jax.shard_map(
        body, mesh=mesh, in_specs=placed, out_specs=P(None, "lat", "lon"), check_vma=False
    )
```

```python
import functools

import jax
import jax.numpy as jnp
from jax import lax
from jax.experimental import pallas as pl
from jax.experimental.pallas import tpu as pltpu
from jax.sharding import PartitionSpec as P

PASSES = 8
MESH = pl.DeviceIdType.MESH
F32 = jnp.float32
BF16 = jnp.bfloat16


def pieces_of(x):
    first = x.astype(BF16)
    rest = x - first.astype(F32)
    second = rest.astype(BF16)
    third = (rest - second.astype(F32)).astype(BF16)
    return first, second, third


def kernel(
    n_lon, n_lat,
    state_ref, coef_lon_ref, coef_lat_ref, land_ref, cols_ref, count_ref, value_ref, weight_ref,
    out_ref,
    recv, seen, hot, spread, spread_bf, pieces, scattered, coefs, coef_out, coef_west, coef_east,
    east_b, west_b, north_b, field, edge_out, edge_west, edge_east,
    own_sem, send_sem, recv_sem, csend_sem, crecv_sem, gsend_sem, grecv_sem,
):
    levels, rows, cols = state_ref.shape
    halo = PASSES
    ext = rows + 2 * halo
    lanes = cols + 128
    cap = recv.shape[3]
    lon = lax.axis_index("lon")
    lat = lax.axis_index("lat")
    east, west = lax.rem(lon + 1, n_lon), lax.rem(lon + n_lon - 1, n_lon)
    north, south = lax.rem(lat + 1, n_lat), lax.rem(lat + n_lat - 1, n_lat)

    def at(lon_to, lat_to):
        return {"lon": lon_to, "lat": lat_to}

    around = [
        at(lon, north), at(lon, south), at(east, lat), at(west, lat),
        at(east, north), at(west, north), at(east, south), at(west, south),
    ]
    barrier = pltpu.get_barrier_semaphore()
    for step in range(1, n_lon):
        pl.semaphore_signal(
            barrier, inc=1, device_id=at(lax.rem(lon + step, n_lon), lat), device_id_type=MESH
        )
    for place in (0, 1, 4, 5, 6, 7):
        pl.semaphore_signal(barrier, inc=1, device_id=around[place], device_id_type=MESH)
    pl.semaphore_wait(barrier, n_lon - 1 + 6)

    sources = (value_ref, weight_ref)

    def profile_copy(which, step):
        peer = lax.rem(lon + step, n_lon)
        start = pl.multiple_of(peer * cap, 128)
        return pltpu.make_async_remote_copy(
            src_ref=sources[which].at[:, pl.ds(start, cap)],
            dst_ref=recv.at[which, step],
            send_sem=send_sem.at[which, step],
            recv_sem=recv_sem.at[which, step],
            device_id=at(peer, lat),
            device_id_type=MESH,
        )

    half = n_lon // 2
    order = []
    for off in range(half, 0, -1):
        order += [off] if 2 * off == n_lon else [off, n_lon - off]
    for step in order:
        for which in (0, 1):
            profile_copy(which, step).start()
    own = [
        pltpu.make_async_copy(
            sources[which].at[:, pl.ds(pl.multiple_of(lon * cap, 128), cap)],
            recv.at[which, 0],
            own_sem.at[which],
        )
        for which in (0, 1)
    ]
    for copy in own:
        copy.start()

    here = pl.ds(halo, rows)
    coefs[0, here, 0:cols] = land_ref[...].astype(F32)
    coefs[1, here, 0:cols] = coef_lon_ref[...]
    coefs[2, here, 0:cols] = coef_lat_ref[...]
    lane = lax.broadcasted_iota(jnp.int32, (rows, 128), 1)
    to_east = jnp.zeros((rows, 128), F32)
    to_west = jnp.zeros((rows, 128), F32)
    for a in range(3):
        low = coefs[a, here, 0:128]
        high = coefs[a, here, cols - 128:cols]
        mine = (lane >= 8 * a) & (lane < 8 * a + 8)
        to_east = jnp.where(mine, pltpu.roll(high, (8 * a + 8) % 128, axis=1), to_east)
        to_west = jnp.where(mine, low if a == 0 else pltpu.roll(low, 8 * a, axis=1), to_west)
    coef_out[0] = to_east
    coef_out[1] = to_west
    top, bottom = pl.ds(rows - halo, halo), pl.ds(0, halo)
    low_rim, high_rim = pl.ds(0, halo), pl.ds(halo + rows, halo)
    coef_moves = [
        (coefs.at[:, pl.ds(rows, halo), 0:cols], coefs.at[:, low_rim, 0:cols]),
        (coefs.at[:, pl.ds(halo, halo), 0:cols], coefs.at[:, high_rim, 0:cols]),
        (coef_out.at[0], coef_west.at[here]),
        (coef_out.at[1], coef_east.at[here]),
        (coef_out.at[0, top], coef_west.at[low_rim]),
        (coef_out.at[1, top], coef_east.at[low_rim]),
        (coef_out.at[0, bottom], coef_west.at[high_rim]),
        (coef_out.at[1, bottom], coef_east.at[high_rim]),
    ]
    coef_copies = [
        pltpu.make_async_remote_copy(
            src_ref=src, dst_ref=dst, send_sem=csend_sem.at[i], recv_sem=crecv_sem.at[i],
            device_id=around[i], device_id_type=MESH,
        )
        for i, (src, dst) in enumerate(coef_moves)
    ]
    for copy in coef_copies:
        copy.start()

    for r in range(rows):
        parts = pieces_of(state_ref[:, r, :])
        for i in range(3):
            pieces[i, levels * r:levels * (r + 1), :] = parts[i]

    def places(step):
        holder = lax.rem(lon + n_lon - step, n_lon)
        entry = cols_ref[:, pl.ds(pl.multiple_of(holder * cap, 128), cap)]
        return holder, lax.shift_right_logical(entry, cols.bit_length() - 1), entry & (cols - 1)

    def gather_step(step, carry):
        _, row, col = places(step)
        which_col = lax.broadcasted_iota(jnp.int32, (cols, cap), 0)
        one_hot = jnp.where(which_col == col, 1.0, 0.0).astype(BF16)
        hot[step] = one_hot
        picked = jnp.dot(pieces[0], one_hot, preferred_element_type=F32)
        picked += jnp.dot(pieces[1], one_hot, preferred_element_type=F32)
        picked += jnp.dot(pieces[2], one_hot, preferred_element_type=F32)
        spread[...] = picked
        row_b = jnp.broadcast_to(row, (levels, cap))
        total = jnp.zeros((levels, cap), F32)
        for r in range(rows):
            total += jnp.where(row_b == r, spread[levels * r:levels * (r + 1), :], 0.0)
        seen[step] = total
        return carry

    lax.fori_loop(0, n_lon, gather_step, 0)

    for copy in coef_copies:
        copy.wait()
    lane_e = lax.broadcasted_iota(jnp.int32, (ext, 128), 1)
    from_west, from_east = coef_west[...], coef_east[...]
    for a in range(3):
        eastern = from_east if a == 0 else pltpu.roll(from_east, 128 - 8 * a, axis=1)
        western = pltpu.roll(from_west, 120 - 8 * a, axis=1)
        coefs[a, :, cols:lanes] = jnp.where(
            lane_e < 8, eastern, jnp.where(lane_e >= 120, western, 0.0)
        )
    row_place = lax.broadcasted_iota(jnp.int32, (ext, lanes), 0)
    first_out = jnp.where(lat == 0, halo, 0)
    last_out = jnp.where(lat == n_lat - 1, halo + rows, ext)
    inside = (row_place >= first_out) & (row_place < last_out)
    sea = jnp.where(inside, coefs[0], 0.0)
    coefs[0] = sea
    east_face = coefs[1] * sea * pltpu.roll(sea, lanes - 1, axis=1)
    north_face = coefs[2] * sea * pltpu.roll(sea, ext - 1, axis=0)
    west_face = pltpu.roll(east_face, 1, axis=1)
    for e in range(ext):
        west_b[e] = jnp.broadcast_to(west_face[e:e + 1, :], (8, lanes))
        east_b[e] = jnp.broadcast_to(east_face[e:e + 1, :], (8, lanes))
        north_b[e] = jnp.broadcast_to(north_face[e:e + 1, :], (8, lanes))

    scattered[...] = jnp.zeros_like(scattered)

    def scatter_step(turn, carry):
        step = jnp.where(turn % 2 == 1, (turn + 1) // 2, (n_lon - turn // 2) % n_lon)
        holder, row, _ = places(step)
        for which in (0, 1):

            @pl.when(step == 0)
            def _():
                own[which].wait()

            @pl.when(step != 0)
            def _():
                profile_copy(which, step).wait_recv()

        slot = lax.broadcasted_iota(jnp.int32, (levels, cap), 1)
        usable = jnp.where(slot < count_ref[0, holder], 1.0, 0.0)
        weighted = recv[1, step] * (recv[0, step] - seen[step]) * usable
        parts = pieces_of(weighted)
        row_b = jnp.broadcast_to(row, (levels, cap))
        for r in range(rows):
            mine = jnp.where(row_b == r, 1.0, 0.0).astype(BF16)
            for i in range(3):
                spread_bf[i, levels * r:levels * (r + 1), :] = mine * parts[i]
        one_hot = hot[step]
        dims = (((1,), (1,)), ((), ()))
        total = lax.dot_general(spread_bf[0], one_hot, dims, preferred_element_type=F32)
        total += lax.dot_general(spread_bf[1], one_hot, dims, preferred_element_type=F32)
        total += lax.dot_general(spread_bf[2], one_hot, dims, preferred_element_type=F32)
        scattered[...] += total
        return carry

    lax.fori_loop(0, n_lon, scatter_step, 0)

    for r in range(rows):
        sea_r = jnp.broadcast_to(coefs[0, halo + r:halo + r + 1, 0:cols], (levels, cols))
        field[0, halo + r, :, 0:cols] = scattered[levels * r:levels * (r + 1), :] * sea_r
    group = 128 // halo
    blocks = rows // group
    lane_g = lax.broadcasted_iota(jnp.int32, (levels, 128), 1)
    for j in range(blocks):
        to_east = jnp.zeros((levels, 128), F32)
        to_west = jnp.zeros((levels, 128), F32)
        for k in range(group):
            low = field[0, halo + j * group + k, :, 0:128]
            high = field[0, halo + j * group + k, :, cols - 128:cols]
            mine = (lane_g >= 8 * k) & (lane_g < 8 * k + 8)
            to_east = jnp.where(mine, pltpu.roll(high, (8 * k + 8) % 128, axis=1) if k < group - 1 else high, to_east)
            to_west = jnp.where(mine, low if k == 0 else pltpu.roll(low, 8 * k, axis=1), to_west)
        edge_out[0, j] = to_east
        edge_out[1, j] = to_west
    middle = pl.ds(1, blocks)
    field_moves = [
        (field.at[0, pl.ds(rows, halo), :, 0:cols], field.at[0, low_rim, :, 0:cols]),
        (field.at[0, pl.ds(halo, halo), :, 0:cols], field.at[0, high_rim, :, 0:cols]),
        (edge_out.at[0], edge_west.at[middle]),
        (edge_out.at[1], edge_east.at[middle]),
        (edge_out.at[0, blocks - 1], edge_west.at[0]),
        (edge_out.at[1, blocks - 1], edge_east.at[0]),
        (edge_out.at[0, 0], edge_west.at[blocks + 1]),
        (edge_out.at[1, 0], edge_east.at[blocks + 1]),
    ]
    field_copies = [
        pltpu.make_async_remote_copy(
            src_ref=src, dst_ref=dst, send_sem=gsend_sem.at[i], recv_sem=grecv_sem.at[i],
            device_id=around[i], device_id_type=MESH,
        )
        for i, (src, dst) in enumerate(field_moves)
    ]
    for i in (2, 3, 0, 1, 4, 5, 6, 7):
        field_copies[i].start()

    def unpack(first, last):
        for e in range(first, last):
            j, k = (e + halo) // group, (e + halo) % group
            eastern = edge_east[j]
            if k > 0:
                eastern = pltpu.roll(eastern, 128 - 8 * k, axis=1)
            western = edge_west[j]
            if k < group - 1:
                western = pltpu.roll(western, 120 - 8 * k, axis=1)
            field[0, e, :, cols:lanes] = jnp.where(
                lane_g < 8, eastern, jnp.where(lane_g >= 120, western, 0.0)
            )

    def twice(face):
        return jnp.concatenate([face] * (levels // 8), axis=0)

    def advance(t, first, last):
        g = field[t - 1, first]
        flux_south = twice(north_b[first - 1]) * (g - field[t - 1, first - 1])
        for e in range(first, last):
            g_north = field[t - 1, e + 1]
            flux_north = twice(north_b[e]) * (g_north - g)
            flux_east = twice(east_b[e]) * (pltpu.roll(g, lanes - 1, axis=1) - g)
            flux_west = twice(west_b[e]) * (g - pltpu.roll(g, 1, axis=1))
            new = g + flux_east - flux_west + flux_north - flux_south
            if t == PASSES:
                out_ref[e - halo] = new[:, 0:cols]
            else:
                field[t, e] = new
            g, flux_south = g_north, flux_north

    field_copies[2].wait_recv()
    field_copies[3].wait_recv()
    unpack(halo, halo + rows)
    for t in range(1, PASSES + 1):
        advance(t, halo + t, halo + rows - t)
    for i in (0, 1, 4, 5, 6, 7):
        field_copies[i].wait_recv()
    unpack(0, halo)
    unpack(halo + rows, ext)
    for t in range(1, PASSES + 1):
        advance(t, t, halo + t)
        advance(t, halo + rows - t, ext - t)

    for step in order:
        for which in (0, 1):
            profile_copy(which, step).wait_send()
    for copy in field_copies:
        copy.wait_send()


def body(state, coef_lon, coef_lat, land_sea, send_cols, send_count, obs_value, obs_weight):
    levels, rows, cols = state.shape
    n_lon = lax.axis_size("lon")
    n_lat = lax.axis_size("lat")
    slots = send_cols.shape[1]
    cap = slots // n_lon
    ext, lanes = rows + 2 * PASSES, cols + 128
    blocks = rows * PASSES // 128
    vmem = pl.BlockSpec(memory_space=pltpu.VMEM)
    anywhere = pl.BlockSpec(memory_space=pl.ANY)
    dma = pltpu.SemaphoreType.DMA
    out = pl.pallas_call(
        functools.partial(kernel, n_lon, n_lat),
        out_shape=jax.ShapeDtypeStruct((rows, levels, cols), F32),
        in_specs=[vmem] * 5 + [pl.BlockSpec(memory_space=pltpu.SMEM)] + [anywhere] * 2,
        out_specs=vmem,
        scratch_shapes=[
            pltpu.VMEM((2, n_lon, levels, cap), F32),
            pltpu.VMEM((n_lon, levels, cap), F32),
            pltpu.VMEM((n_lon, cols, cap), BF16),
            pltpu.VMEM((rows * levels, cap), F32),
            pltpu.VMEM((3, rows * levels, cap), BF16),
            pltpu.VMEM((3, rows * levels, cols), BF16),
            pltpu.VMEM((rows * levels, cols), F32),
            pltpu.VMEM((3, ext, lanes), F32),
            pltpu.VMEM((2, rows, 128), F32),
            pltpu.VMEM((ext, 128), F32),
            pltpu.VMEM((ext, 128), F32),
            pltpu.VMEM((ext, 8, lanes), F32),
            pltpu.VMEM((ext, 8, lanes), F32),
            pltpu.VMEM((ext, 8, lanes), F32),
            pltpu.VMEM((PASSES, ext, levels, lanes), F32),
            pltpu.VMEM((2, blocks, levels, 128), F32),
            pltpu.VMEM((blocks + 2, levels, 128), F32),
            pltpu.VMEM((blocks + 2, levels, 128), F32),
            dma((2,)),
            dma((2, n_lon)),
            dma((2, n_lon)),
            dma((8,)),
            dma((8,)),
            dma((8,)),
            dma((8,)),
        ],
        compiler_params=pltpu.CompilerParams(
            collective_id=0, has_side_effects=True, vmem_limit_bytes=48 * 2**20
        ),
        name="analysis",
    )(
        state, coef_lon, coef_lat, land_sea, send_cols, send_count,
        obs_value.reshape(levels, slots), obs_weight.reshape(levels, slots),
    )
    return jnp.transpose(out, (1, 0, 2))


def solution(mesh):
    placed = (
        P(None, "lat", "lon"),
        P("lat", "lon"),
        P("lat", "lon"),
        P("lat", "lon"),
        P("lat", "lon"),
        P("lat", "lon"),
        P(None, "lat", "lon"),
        P(None, "lat", "lon"),
    )
    return jax.shard_map(
        body, mesh=mesh, in_specs=placed, out_specs=P(None, "lat", "lon"), check_vma=False
    )
```

```python
import functools

import jax
import jax.numpy as jnp
from jax import lax
from jax.experimental import pallas as pl
from jax.experimental.pallas import tpu as pltpu
from jax.sharding import PartitionSpec as P

PASSES = 8
MESH = pl.DeviceIdType.MESH
F32 = jnp.float32
BF16 = jnp.bfloat16


def pieces_of(x):
    first = x.astype(BF16)
    rest = x - first.astype(F32)
    second = rest.astype(BF16)
    third = (rest - second.astype(F32)).astype(BF16)
    return first, second, third


def kernel(
    n_lon, n_lat,
    state_ref, coef_lon_ref, coef_lat_ref, land_ref, cols_ref, count_ref, value_ref, weight_ref,
    out_ref,
    recv, seen, hot, spread, spread_bf, pieces, scattered, coefs, coef_out, coef_west, coef_east,
    east_b, west_b, north_b, field, edge_out, edge_west, edge_east,
    own_sem, send_sem, recv_sem, csend_sem, crecv_sem, gsend_sem, grecv_sem,
):
    levels, rows, cols = state_ref.shape
    cells = rows * levels
    halo = PASSES
    ext = rows + 2 * halo
    lanes = cols + 128
    cap = recv.shape[4]
    lon = lax.axis_index("lon")
    lat = lax.axis_index("lat")
    east, west = lax.rem(lon + 1, n_lon), lax.rem(lon + n_lon - 1, n_lon)
    north, south = lax.rem(lat + 1, n_lat), lax.rem(lat + n_lat - 1, n_lat)

    def at(lon_to, lat_to):
        return {"lon": lon_to, "lat": lat_to}

    around = [
        at(lon, north), at(lon, south), at(east, lat), at(west, lat),
        at(east, north), at(west, north), at(east, south), at(west, south),
    ]
    barrier = pltpu.get_barrier_semaphore()
    for step in range(1, n_lon):
        pl.semaphore_signal(
            barrier, inc=1, device_id=at(lax.rem(lon + step, n_lon), lat), device_id_type=MESH
        )
    for place in (0, 1, 4, 5, 6, 7):
        pl.semaphore_signal(barrier, inc=1, device_id=around[place], device_id_type=MESH)

    here = pl.ds(halo, rows)
    coefs[0, here, 0:cols] = land_ref[...].astype(F32)
    coefs[1, here, 0:cols] = coef_lon_ref[...]
    coefs[2, here, 0:cols] = coef_lat_ref[...]
    lane = lax.broadcasted_iota(jnp.int32, (rows, 128), 1)
    to_east = jnp.zeros((rows, 128), F32)
    to_west = jnp.zeros((rows, 128), F32)
    for a in range(3):
        low = coefs[a, here, 0:128]
        high = coefs[a, here, cols - 128:cols]
        mine = (lane >= 8 * a) & (lane < 8 * a + 8)
        to_east = jnp.where(mine, pltpu.roll(high, (8 * a + 8) % 128, axis=1), to_east)
        to_west = jnp.where(mine, low if a == 0 else pltpu.roll(low, 8 * a, axis=1), to_west)
    coef_out[0] = to_east
    coef_out[1] = to_west

    for r in range(rows):
        parts = pieces_of(state_ref[:, r, :])
        for i in range(3):
            pieces[cells * i + levels * r:cells * i + levels * (r + 1), :] = parts[i]

    pl.semaphore_wait(barrier, n_lon - 1 + 6)

    sources = (value_ref, weight_ref)

    def profile_copy(which, step):
        peer = lax.rem(lon + step, n_lon)
        start = pl.multiple_of(peer * cap, 128)
        return pltpu.make_async_remote_copy(
            src_ref=sources[which].at[:, :, pl.ds(start, cap)],
            dst_ref=recv.at[which, step],
            send_sem=send_sem.at[which, step],
            recv_sem=recv_sem.at[which, step],
            device_id=at(peer, lat),
            device_id_type=MESH,
        )

    half = n_lon // 2
    order = []
    for off in range(half, 0, -1):
        order += [off] if 2 * off == n_lon else [off, n_lon - off]
    for step in order:
        for which in (0, 1):
            profile_copy(which, step).start()
    own = [
        pltpu.make_async_copy(
            sources[which].at[:, :, pl.ds(pl.multiple_of(lon * cap, 128), cap)],
            recv.at[which, 0],
            own_sem.at[which],
        )
        for which in (0, 1)
    ]
    for copy in own:
        copy.start()

    top, bottom = pl.ds(rows - halo, halo), pl.ds(0, halo)
    low_rim, high_rim = pl.ds(0, halo), pl.ds(halo + rows, halo)
    coef_moves = [
        (coefs.at[:, pl.ds(rows, halo), 0:cols], coefs.at[:, low_rim, 0:cols]),
        (coefs.at[:, pl.ds(halo, halo), 0:cols], coefs.at[:, high_rim, 0:cols]),
        (coef_out.at[0], coef_west.at[here]),
        (coef_out.at[1], coef_east.at[here]),
        (coef_out.at[0, top], coef_west.at[low_rim]),
        (coef_out.at[1, top], coef_east.at[low_rim]),
        (coef_out.at[0, bottom], coef_west.at[high_rim]),
        (coef_out.at[1, bottom], coef_east.at[high_rim]),
    ]
    coef_copies = [
        pltpu.make_async_remote_copy(
            src_ref=src, dst_ref=dst, send_sem=csend_sem.at[i], recv_sem=crecv_sem.at[i],
            device_id=around[i], device_id_type=MESH,
        )
        for i, (src, dst) in enumerate(coef_moves)
    ]
    for copy in coef_copies:
        copy.start()

    def places(step):
        holder = lax.rem(lon + n_lon - step, n_lon)
        entry = cols_ref[:, pl.ds(pl.multiple_of(holder * cap, 128), cap)]
        return holder, lax.shift_right_logical(entry, cols.bit_length() - 1), entry & (cols - 1)

    def gather_step(step, carry):
        _, row, col = places(step)
        which_col = lax.broadcasted_iota(jnp.int32, (cols, cap), 0)
        one_hot = jnp.where(which_col == col, 1.0, 0.0).astype(BF16)
        hot[step] = one_hot
        spread[...] = jnp.dot(pieces[...], one_hot, preferred_element_type=F32)
        row_b = jnp.broadcast_to(row, (8, cap))
        totals = [jnp.zeros((8, cap), F32) for _ in range(0, levels, 8)]
        for r in range(rows):
            mine = row_b == r
            for h in range(levels // 8):
                at_row = pl.ds(levels * r + 8 * h, 8)
                picked = spread[at_row, :]
                for i in range(1, 3):
                    picked += spread[pl.ds(cells * i + levels * r + 8 * h, 8), :]
                totals[h] += jnp.where(mine, picked, 0.0)
        for h in range(levels // 8):
            seen[step, 8 * h:8 * h + 8] = totals[h]
        return carry

    lax.fori_loop(0, n_lon, gather_step, 0)

    for copy in coef_copies:
        copy.wait()
    lane_e = lax.broadcasted_iota(jnp.int32, (ext, 128), 1)
    from_west, from_east = coef_west[...], coef_east[...]
    for a in range(3):
        eastern = from_east if a == 0 else pltpu.roll(from_east, 128 - 8 * a, axis=1)
        western = pltpu.roll(from_west, 120 - 8 * a, axis=1)
        coefs[a, :, cols:lanes] = jnp.where(
            lane_e < 8, eastern, jnp.where(lane_e >= 120, western, 0.0)
        )
    row_place = lax.broadcasted_iota(jnp.int32, (ext, lanes), 0)
    first_out = jnp.where(lat == 0, halo, 0)
    last_out = jnp.where(lat == n_lat - 1, halo + rows, ext)
    inside = (row_place >= first_out) & (row_place < last_out)
    sea = jnp.where(inside, coefs[0], 0.0)
    coefs[0] = sea
    east_face = coefs[1] * sea * pltpu.roll(sea, lanes - 1, axis=1)
    north_face = coefs[2] * sea * pltpu.roll(sea, ext - 1, axis=0)
    west_face = pltpu.roll(east_face, 1, axis=1)
    for e in range(ext):
        west_b[e] = jnp.broadcast_to(west_face[e:e + 1, :], (8, lanes))
        east_b[e] = jnp.broadcast_to(east_face[e:e + 1, :], (8, lanes))
        north_b[e] = jnp.broadcast_to(north_face[e:e + 1, :], (8, lanes))

    scattered[...] = jnp.zeros_like(scattered)

    def scatter_step(turn, carry):
        step = jnp.where(turn % 2 == 1, (turn + 1) // 2, (n_lon - turn // 2) % n_lon)
        holder, row, _ = places(step)
        for which in (0, 1):

            @pl.when(step == 0)
            def _():
                own[which].wait()

            @pl.when(step != 0)
            def _():
                profile_copy(which, step).wait_recv()

        slot = lax.broadcasted_iota(jnp.int32, (levels, cap), 1)
        usable = jnp.where(slot < count_ref[0, holder], 1.0, 0.0)
        weighted = recv[1, step, :, 0, :] * (recv[0, step, :, 0, :] - seen[step]) * usable
        parts = pieces_of(weighted)[:2]
        row_b = jnp.broadcast_to(row.astype(F32), (levels, cap)).astype(BF16)
        nothing = jnp.zeros((levels, cap), BF16)
        for r in range(rows):
            mine = row_b == jnp.asarray(r, BF16)
            for i in range(2):
                start = cells * i + levels * r
                spread_bf[start:start + levels, :] = jnp.where(mine, parts[i], nothing)
        total = lax.dot_general(
            spread_bf[...], hot[step], (((1,), (1,)), ((), ())), preferred_element_type=F32
        )
        scattered[...] += total[:cells] + total[cells:]
        return carry

    lax.fori_loop(0, n_lon, scatter_step, 0)

    group = 128 // halo
    blocks = rows // group
    middle = pl.ds(1, blocks)
    field_moves = [
        (field.at[0, pl.ds(rows, halo), :, 0:cols], field.at[0, low_rim, :, 0:cols]),
        (field.at[0, pl.ds(halo, halo), :, 0:cols], field.at[0, high_rim, :, 0:cols]),
        (edge_out.at[0], edge_west.at[middle]),
        (edge_out.at[1], edge_east.at[middle]),
        (edge_out.at[0, blocks - 1], edge_west.at[0]),
        (edge_out.at[1, blocks - 1], edge_east.at[0]),
        (edge_out.at[0, 0], edge_west.at[blocks + 1]),
        (edge_out.at[1, 0], edge_east.at[blocks + 1]),
    ]
    field_copies = [
        pltpu.make_async_remote_copy(
            src_ref=src, dst_ref=dst, send_sem=gsend_sem.at[i], recv_sem=grecv_sem.at[i],
            device_id=around[i], device_id_type=MESH,
        )
        for i, (src, dst) in enumerate(field_moves)
    ]
    border = list(range(halo)) + list(range(rows - halo, rows))
    for r in border + list(range(halo, rows - halo)):
        if r == halo:
            field_copies[0].start()
            field_copies[1].start()
        sea_r = jnp.broadcast_to(coefs[0, halo + r:halo + r + 1, 0:cols], (levels, cols))
        field[0, halo + r, :, 0:cols] = scattered[levels * r:levels * (r + 1), :] * sea_r
    lane_g = lax.broadcasted_iota(jnp.int32, (levels, 128), 1)
    for j in range(blocks):
        to_east = jnp.zeros((levels, 128), F32)
        to_west = jnp.zeros((levels, 128), F32)
        for k in range(group):
            low = field[0, halo + j * group + k, :, 0:128]
            high = field[0, halo + j * group + k, :, cols - 128:cols]
            mine = (lane_g >= 8 * k) & (lane_g < 8 * k + 8)
            to_east = jnp.where(mine, pltpu.roll(high, (8 * k + 8) % 128, axis=1) if k < group - 1 else high, to_east)
            to_west = jnp.where(mine, low if k == 0 else pltpu.roll(low, 8 * k, axis=1), to_west)
        edge_out[0, j] = to_east
        edge_out[1, j] = to_west
    for i in range(2, 8):
        field_copies[i].start()

    def unpack(first, last):
        for e in range(first, last):
            j, k = (e + halo) // group, (e + halo) % group
            eastern = edge_east[j]
            if k > 0:
                eastern = pltpu.roll(eastern, 128 - 8 * k, axis=1)
            western = edge_west[j]
            if k < group - 1:
                western = pltpu.roll(western, 120 - 8 * k, axis=1)
            field[0, e, :, cols:lanes] = jnp.where(
                lane_g < 8, eastern, jnp.where(lane_g >= 120, western, 0.0)
            )

    def twice(face):
        return jnp.concatenate([face] * (levels // 8), axis=0)

    def advance(t, first, last):
        g = field[t - 1, first]
        flux_south = twice(north_b[first - 1]) * (g - field[t - 1, first - 1])
        for e in range(first, last):
            g_north = field[t - 1, e + 1]
            flux_north = twice(north_b[e]) * (g_north - g)
            flux_east = twice(east_b[e]) * (pltpu.roll(g, lanes - 1, axis=1) - g)
            flux_west = twice(west_b[e]) * (g - pltpu.roll(g, 1, axis=1))
            new = g + flux_east - flux_west + flux_north - flux_south
            if t == PASSES:
                out_ref[e - halo] = new[:, 0:cols]
            else:
                field[t, e] = new
            g, flux_south = g_north, flux_north

    field_copies[2].wait_recv()
    field_copies[3].wait_recv()
    unpack(halo, halo + rows)
    for t in range(1, PASSES + 1):
        advance(t, halo + t, halo + rows - t)
    for i in (0, 1, 4, 5, 6, 7):
        field_copies[i].wait_recv()
    unpack(0, halo)
    unpack(halo + rows, ext)
    for t in range(1, PASSES + 1):
        advance(t, t, halo + t)
        advance(t, halo + rows - t, ext - t)

    for step in order:
        for which in (0, 1):
            profile_copy(which, step).wait_send()
    for copy in field_copies:
        copy.wait_send()


def body(state, coef_lon, coef_lat, land_sea, send_cols, send_count, obs_value, obs_weight):
    levels, rows, cols = state.shape
    n_lon = lax.axis_size("lon")
    n_lat = lax.axis_size("lat")
    slots = send_cols.shape[1]
    cap = slots // n_lon
    ext, lanes = rows + 2 * PASSES, cols + 128
    blocks = rows * PASSES // 128
    vmem = pl.BlockSpec(memory_space=pltpu.VMEM)
    anywhere = pl.BlockSpec(memory_space=pl.ANY)
    dma = pltpu.SemaphoreType.DMA
    out = pl.pallas_call(
        functools.partial(kernel, n_lon, n_lat),
        out_shape=jax.ShapeDtypeStruct((rows, levels, cols), F32),
        in_specs=[vmem] * 5 + [pl.BlockSpec(memory_space=pltpu.SMEM)] + [anywhere] * 2,
        out_specs=vmem,
        scratch_shapes=[
            pltpu.VMEM((2, n_lon, levels, 1, cap), F32),
            pltpu.VMEM((n_lon, levels, cap), F32),
            pltpu.VMEM((n_lon, cols, cap), BF16),
            pltpu.VMEM((3 * rows * levels, cap), F32),
            pltpu.VMEM((2 * rows * levels, cap), BF16),
            pltpu.VMEM((3 * rows * levels, cols), BF16),
            pltpu.VMEM((rows * levels, cols), F32),
            pltpu.VMEM((3, ext, lanes), F32),
            pltpu.VMEM((2, rows, 128), F32),
            pltpu.VMEM((ext, 128), F32),
            pltpu.VMEM((ext, 128), F32),
            pltpu.VMEM((ext, 8, lanes), F32),
            pltpu.VMEM((ext, 8, lanes), F32),
            pltpu.VMEM((ext, 8, lanes), F32),
            pltpu.VMEM((PASSES, ext, levels, lanes), F32),
            pltpu.VMEM((2, blocks, levels, 128), F32),
            pltpu.VMEM((blocks + 2, levels, 128), F32),
            pltpu.VMEM((blocks + 2, levels, 128), F32),
            dma((2,)),
            dma((2, n_lon)),
            dma((2, n_lon)),
            dma((8,)),
            dma((8,)),
            dma((8,)),
            dma((8,)),
        ],
        compiler_params=pltpu.CompilerParams(
            collective_id=0, has_side_effects=True, vmem_limit_bytes=48 * 2**20
        ),
        name="analysis",
    )(
        state, coef_lon, coef_lat, land_sea, send_cols, send_count,
        obs_value, obs_weight,
    )
    return jnp.transpose(out, (1, 0, 2))


def solution(mesh):
    placed = (
        P(None, "lat", "lon"),
        P("lat", "lon"),
        P("lat", "lon"),
        P("lat", "lon"),
        P("lat", "lon"),
        P("lat", "lon"),
        P(None, "lat", "lon"),
        P(None, "lat", "lon"),
    )
    return jax.shard_map(
        body, mesh=mesh, in_specs=placed, out_specs=P(None, "lat", "lon"), check_vma=False
    )
```

```python
import functools

import jax
import jax.numpy as jnp
from jax import lax
from jax.experimental import pallas as pl
from jax.experimental.pallas import tpu as pltpu
from jax.sharding import PartitionSpec as P

PASSES = 8
MESH = pl.DeviceIdType.MESH
F32 = jnp.float32
BF16 = jnp.bfloat16


def pieces_of(x):
    first = x.astype(BF16)
    rest = x - first.astype(F32)
    second = rest.astype(BF16)
    third = (rest - second.astype(F32)).astype(BF16)
    return first, second, third


def kernel(
    n_lon, n_lat,
    state_in, coef_lon_in, coef_lat_in, land_in, cols_in, count_in, value_in, weight_in,
    out_ref,
    state_ref, coef_lon_ref, coef_lat_ref, land_ref, cols_ref, count_ref, value_ref, weight_ref,
    outgoing,    recv, seen, hot, spread, spread_bf, pieces, scattered, coefs, coef_out, coef_west, coef_east,
    east_b, west_b, north_b, field, edge_out, edge_west, edge_east,
    load_sem, send_sem, recv_sem, csend_sem, crecv_sem, gsend_sem, grecv_sem,
):
    levels, rows, cols = state_ref.shape
    cells = rows * levels
    halo = PASSES
    ext = rows + 2 * halo
    lanes = cols + 128
    cap = recv.shape[3]
    lon = lax.axis_index("lon")
    lat = lax.axis_index("lat")
    east, west = lax.rem(lon + 1, n_lon), lax.rem(lon + n_lon - 1, n_lon)
    north, south = lax.rem(lat + 1, n_lat), lax.rem(lat + n_lat - 1, n_lat)

    def at(lon_to, lat_to):
        return {"lon": lon_to, "lat": lat_to}

    around = [
        at(lon, north), at(lon, south), at(east, lat), at(west, lat),
        at(east, north), at(west, north), at(east, south), at(west, south),
    ]
    loads = [
        pltpu.make_async_copy(src, dst, load_sem.at[i])
        for i, (src, dst) in enumerate((
            (value_in, value_ref), (weight_in, weight_ref), (state_in, state_ref),
            (coef_lon_in, coef_lon_ref), (coef_lat_in, coef_lat_ref), (land_in, land_ref),
            (cols_in, cols_ref), (count_in, count_ref),
        ))
    ]
    for load in loads:
        load.start()
    barrier = pltpu.get_barrier_semaphore()
    for step in range(1, n_lon):
        pl.semaphore_signal(
            barrier, inc=1, device_id=at(lax.rem(lon + step, n_lon), lat), device_id_type=MESH
        )
    for place in (0, 1, 4, 5, 6, 7):
        pl.semaphore_signal(barrier, inc=1, device_id=around[place], device_id_type=MESH)

    loads[0].wait()
    loads[1].wait()
    for peer in range(n_lon):
        outgoing[peer, 0] = value_ref[:, 0, peer * cap:(peer + 1) * cap]
        outgoing[peer, 1] = weight_ref[:, 0, peer * cap:(peer + 1) * cap]
    pl.semaphore_wait(barrier, n_lon - 1 + 6)

    def profile_copy(step):
        peer = lax.rem(lon + step, n_lon)
        return pltpu.make_async_remote_copy(
            src_ref=outgoing.at[peer],
            dst_ref=recv.at[step],
            send_sem=send_sem.at[step],
            recv_sem=recv_sem.at[step],
            device_id=at(peer, lat),
            device_id_type=MESH,
        )

    half = n_lon // 2
    order = []
    for off in range(half, 0, -1):
        order += [off] if 2 * off == n_lon else [off, n_lon - off]
    for step in order:
        profile_copy(step).start()
    recv[0] = outgoing[lon]

    for load in loads[2:]:
        load.wait()
    here = pl.ds(halo, rows)
    coefs[0, here, 0:cols] = land_ref[...].astype(F32)
    coefs[1, here, 0:cols] = coef_lon_ref[...]
    coefs[2, here, 0:cols] = coef_lat_ref[...]
    lane = lax.broadcasted_iota(jnp.int32, (rows, 128), 1)
    to_east = jnp.zeros((rows, 128), F32)
    to_west = jnp.zeros((rows, 128), F32)
    for a in range(3):
        low = coefs[a, here, 0:128]
        high = coefs[a, here, cols - 128:cols]
        mine = (lane >= 8 * a) & (lane < 8 * a + 8)
        to_east = jnp.where(mine, pltpu.roll(high, (8 * a + 8) % 128, axis=1), to_east)
        to_west = jnp.where(mine, low if a == 0 else pltpu.roll(low, 8 * a, axis=1), to_west)
    coef_out[0] = to_east
    coef_out[1] = to_west

    top, bottom = pl.ds(rows - halo, halo), pl.ds(0, halo)
    low_rim, high_rim = pl.ds(0, halo), pl.ds(halo + rows, halo)
    coef_moves = [
        (coefs.at[:, pl.ds(rows, halo), 0:cols], coefs.at[:, low_rim, 0:cols]),
        (coefs.at[:, pl.ds(halo, halo), 0:cols], coefs.at[:, high_rim, 0:cols]),
        (coef_out.at[0], coef_west.at[here]),
        (coef_out.at[1], coef_east.at[here]),
        (coef_out.at[0, top], coef_west.at[low_rim]),
        (coef_out.at[1, top], coef_east.at[low_rim]),
        (coef_out.at[0, bottom], coef_west.at[high_rim]),
        (coef_out.at[1, bottom], coef_east.at[high_rim]),
    ]
    coef_copies = [
        pltpu.make_async_remote_copy(
            src_ref=src, dst_ref=dst, send_sem=csend_sem.at[i], recv_sem=crecv_sem.at[i],
            device_id=around[i], device_id_type=MESH,
        )
        for i, (src, dst) in enumerate(coef_moves)
    ]
    for copy in coef_copies:
        copy.start()

    for r in range(rows):
        parts = pieces_of(state_ref[:, r, :])
        for i in range(3):
            pieces[cells * i + levels * r:cells * i + levels * (r + 1), :] = parts[i]

    def places(step):
        holder = lax.rem(lon + n_lon - step, n_lon)
        entry = cols_ref[:, pl.ds(pl.multiple_of(holder * cap, 128), cap)]
        return holder, lax.shift_right_logical(entry, cols.bit_length() - 1), entry & (cols - 1)

    def gather_step(step, carry):
        _, row, col = places(step)
        which_col = lax.broadcasted_iota(jnp.int32, (cols, cap), 0)
        one_hot = jnp.where(which_col == col, 1.0, 0.0).astype(BF16)
        hot[step] = one_hot
        spread[...] = jnp.dot(pieces[...], one_hot, preferred_element_type=F32)
        row_b = jnp.broadcast_to(row, (8, cap))
        totals = [jnp.zeros((8, cap), F32) for _ in range(0, levels, 8)]
        for r in range(rows):
            mine = row_b == r
            for h in range(levels // 8):
                at_row = pl.ds(levels * r + 8 * h, 8)
                picked = spread[at_row, :]
                for i in range(1, 3):
                    picked += spread[pl.ds(cells * i + levels * r + 8 * h, 8), :]
                totals[h] += jnp.where(mine, picked, 0.0)
        for h in range(levels // 8):
            seen[step, 8 * h:8 * h + 8] = totals[h]
        return carry

    lax.fori_loop(0, n_lon, gather_step, 0)

    for copy in coef_copies:
        copy.wait()
    lane_e = lax.broadcasted_iota(jnp.int32, (ext, 128), 1)
    from_west, from_east = coef_west[...], coef_east[...]
    for a in range(3):
        eastern = from_east if a == 0 else pltpu.roll(from_east, 128 - 8 * a, axis=1)
        western = pltpu.roll(from_west, 120 - 8 * a, axis=1)
        coefs[a, :, cols:lanes] = jnp.where(
            lane_e < 8, eastern, jnp.where(lane_e >= 120, western, 0.0)
        )
    row_place = lax.broadcasted_iota(jnp.int32, (ext, lanes), 0)
    first_out = jnp.where(lat == 0, halo, 0)
    last_out = jnp.where(lat == n_lat - 1, halo + rows, ext)
    inside = (row_place >= first_out) & (row_place < last_out)
    sea = jnp.where(inside, coefs[0], 0.0)
    coefs[0] = sea
    east_face = coefs[1] * sea * pltpu.roll(sea, lanes - 1, axis=1)
    north_face = coefs[2] * sea * pltpu.roll(sea, ext - 1, axis=0)
    west_face = pltpu.roll(east_face, 1, axis=1)
    for e in range(ext):
        west_b[e] = jnp.broadcast_to(west_face[e:e + 1, :], (8, lanes))
        east_b[e] = jnp.broadcast_to(east_face[e:e + 1, :], (8, lanes))
        north_b[e] = jnp.broadcast_to(north_face[e:e + 1, :], (8, lanes))

    scattered[...] = jnp.zeros_like(scattered)

    def scatter_step(turn, carry):
        step = jnp.where(turn % 2 == 1, (turn + 1) // 2, (n_lon - turn // 2) % n_lon)
        holder, row, _ = places(step)

        @pl.when(step != 0)
        def _():
            profile_copy(step).wait_recv()

        slot = lax.broadcasted_iota(jnp.int32, (levels, cap), 1)
        usable = jnp.where(slot < count_ref[0, holder], 1.0, 0.0)
        weighted = recv[step, 1] * (recv[step, 0] - seen[step]) * usable
        parts = pieces_of(weighted)[:2]
        row_b = jnp.broadcast_to(row.astype(F32), (levels, cap)).astype(BF16)
        nothing = jnp.zeros((levels, cap), BF16)
        for r in range(rows):
            mine = row_b == jnp.asarray(r, BF16)
            for i in range(2):
                start = cells * i + levels * r
                spread_bf[start:start + levels, :] = jnp.where(mine, parts[i], nothing)
        total = lax.dot_general(
            spread_bf[...], hot[step], (((1,), (1,)), ((), ())), preferred_element_type=F32
        )
        scattered[...] += total[:cells] + total[cells:]
        return carry

    lax.fori_loop(0, n_lon, scatter_step, 0)

    group = 128 // halo
    blocks = rows // group
    middle = pl.ds(1, blocks)
    field_moves = [
        (field.at[0, pl.ds(rows, halo), :, 0:cols], field.at[0, low_rim, :, 0:cols]),
        (field.at[0, pl.ds(halo, halo), :, 0:cols], field.at[0, high_rim, :, 0:cols]),
        (edge_out.at[0], edge_west.at[middle]),
        (edge_out.at[1], edge_east.at[middle]),
        (edge_out.at[0, blocks - 1], edge_west.at[0]),
        (edge_out.at[1, blocks - 1], edge_east.at[0]),
        (edge_out.at[0, 0], edge_west.at[blocks + 1]),
        (edge_out.at[1, 0], edge_east.at[blocks + 1]),
    ]
    field_copies = [
        pltpu.make_async_remote_copy(
            src_ref=src, dst_ref=dst, send_sem=gsend_sem.at[i], recv_sem=grecv_sem.at[i],
            device_id=around[i], device_id_type=MESH,
        )
        for i, (src, dst) in enumerate(field_moves)
    ]
    border = list(range(halo)) + list(range(rows - halo, rows))
    for r in border + list(range(halo, rows - halo)):
        if r == halo:
            field_copies[0].start()
            field_copies[1].start()
        sea_r = jnp.broadcast_to(coefs[0, halo + r:halo + r + 1, 0:cols], (levels, cols))
        field[0, halo + r, :, 0:cols] = scattered[levels * r:levels * (r + 1), :] * sea_r
    lane_g = lax.broadcasted_iota(jnp.int32, (levels, 128), 1)
    for j in range(blocks):
        to_east = jnp.zeros((levels, 128), F32)
        to_west = jnp.zeros((levels, 128), F32)
        for k in range(group):
            low = field[0, halo + j * group + k, :, 0:128]
            high = field[0, halo + j * group + k, :, cols - 128:cols]
            mine = (lane_g >= 8 * k) & (lane_g < 8 * k + 8)
            to_east = jnp.where(mine, pltpu.roll(high, (8 * k + 8) % 128, axis=1) if k < group - 1 else high, to_east)
            to_west = jnp.where(mine, low if k == 0 else pltpu.roll(low, 8 * k, axis=1), to_west)
        edge_out[0, j] = to_east
        edge_out[1, j] = to_west
    for i in range(2, 8):
        field_copies[i].start()

    def unpack(first, last):
        for e in range(first, last):
            j, k = (e + halo) // group, (e + halo) % group
            eastern = edge_east[j]
            if k > 0:
                eastern = pltpu.roll(eastern, 128 - 8 * k, axis=1)
            western = edge_west[j]
            if k < group - 1:
                western = pltpu.roll(western, 120 - 8 * k, axis=1)
            field[0, e, :, cols:lanes] = jnp.where(
                lane_g < 8, eastern, jnp.where(lane_g >= 120, western, 0.0)
            )

    def twice(face):
        return jnp.concatenate([face] * (levels // 8), axis=0)

    def advance(t, first, last):
        g = field[t - 1, first]
        flux_south = twice(north_b[first - 1]) * (g - field[t - 1, first - 1])
        for e in range(first, last):
            g_north = field[t - 1, e + 1]
            flux_north = twice(north_b[e]) * (g_north - g)
            flux_east = twice(east_b[e]) * (pltpu.roll(g, lanes - 1, axis=1) - g)
            flux_west = twice(west_b[e]) * (g - pltpu.roll(g, 1, axis=1))
            new = g + flux_east - flux_west + flux_north - flux_south
            if t == PASSES:
                out_ref[e - halo] = new[:, 0:cols]
            else:
                field[t, e] = new
            g, flux_south = g_north, flux_north

    field_copies[2].wait_recv()
    field_copies[3].wait_recv()
    unpack(halo, halo + rows)
    for t in range(1, PASSES + 1):
        advance(t, halo + t, halo + rows - t)
    for i in (0, 1, 4, 5, 6, 7):
        field_copies[i].wait_recv()
    unpack(0, halo)
    unpack(halo + rows, ext)
    for t in range(1, PASSES + 1):
        advance(t, t, halo + t)
        advance(t, halo + rows - t, ext - t)

    for step in order:
        profile_copy(step).wait_send()
    for copy in field_copies:
        copy.wait_send()


def body(state, coef_lon, coef_lat, land_sea, send_cols, send_count, obs_value, obs_weight):
    levels, rows, cols = state.shape
    n_lon = lax.axis_size("lon")
    n_lat = lax.axis_size("lat")
    slots = send_cols.shape[1]
    cap = slots // n_lon
    ext, lanes = rows + 2 * PASSES, cols + 128
    blocks = rows * PASSES // 128
    vmem = pl.BlockSpec(memory_space=pltpu.VMEM)
    dma = pltpu.SemaphoreType.DMA
    out = pl.pallas_call(
        functools.partial(kernel, n_lon, n_lat),
        out_shape=jax.ShapeDtypeStruct((rows, levels, cols), F32),
        in_specs=[pl.BlockSpec(memory_space=pltpu.HBM)] * 8,
        out_specs=vmem,
        scratch_shapes=[
            pltpu.VMEM((levels, rows, cols), F32),
            pltpu.VMEM((rows, cols), F32),
            pltpu.VMEM((rows, cols), F32),
            pltpu.VMEM((rows, cols), jnp.int32),
            pltpu.VMEM((1, slots), jnp.int32),
            pltpu.SMEM((1, n_lon), jnp.int32),
            pltpu.VMEM((levels, 1, slots), F32),
            pltpu.VMEM((levels, 1, slots), F32),
            pltpu.VMEM((n_lon, 2, levels, cap), F32),
            pltpu.VMEM((n_lon, 2, levels, cap), F32),
            pltpu.VMEM((n_lon, levels, cap), F32),
            pltpu.VMEM((n_lon, cols, cap), BF16),
            pltpu.VMEM((3 * rows * levels, cap), F32),
            pltpu.VMEM((2 * rows * levels, cap), BF16),
            pltpu.VMEM((3 * rows * levels, cols), BF16),
            pltpu.VMEM((rows * levels, cols), F32),
            pltpu.VMEM((3, ext, lanes), F32),
            pltpu.VMEM((2, rows, 128), F32),
            pltpu.VMEM((ext, 128), F32),
            pltpu.VMEM((ext, 128), F32),
            pltpu.VMEM((ext, 8, lanes), F32),
            pltpu.VMEM((ext, 8, lanes), F32),
            pltpu.VMEM((ext, 8, lanes), F32),
            pltpu.VMEM((PASSES, ext, levels, lanes), F32),
            pltpu.VMEM((2, blocks, levels, 128), F32),
            pltpu.VMEM((blocks + 2, levels, 128), F32),
            pltpu.VMEM((blocks + 2, levels, 128), F32),
            dma((8,)),
            dma((n_lon,)),
            dma((n_lon,)),
            dma((8,)),
            dma((8,)),
            dma((8,)),
            dma((8,)),
        ],
        compiler_params=pltpu.CompilerParams(
            collective_id=0, has_side_effects=True, vmem_limit_bytes=64 * 2**20
        ),
        name="analysis",
    )(
        state, coef_lon, coef_lat, land_sea, send_cols, send_count,
        obs_value, obs_weight,
    )
    return jnp.transpose(out, (1, 0, 2))


def solution(mesh):
    placed = (
        P(None, "lat", "lon"),
        P("lat", "lon"),
        P("lat", "lon"),
        P("lat", "lon"),
        P("lat", "lon"),
        P("lat", "lon"),
        P(None, "lat", "lon"),
        P(None, "lat", "lon"),
    )
    return jax.shard_map(
        body, mesh=mesh, in_specs=placed, out_specs=P(None, "lat", "lon"), check_vma=False
    )
```

```python
import functools

import jax
import jax.numpy as jnp
from jax import lax
from jax.experimental import pallas as pl
from jax.experimental.pallas import tpu as pltpu
from jax.sharding import PartitionSpec as P

PASSES = 8
MESH = pl.DeviceIdType.MESH
F32 = jnp.float32
BF16 = jnp.bfloat16


def pieces_of(x):
    first = x.astype(BF16)
    rest = x - first.astype(F32)
    second = rest.astype(BF16)
    third = (rest - second.astype(F32)).astype(BF16)
    return first, second, third


def kernel(
    n_lon, n_lat,
    state_in, coef_lon_in, coef_lat_in, land_in, cols_in, count_in, value_in, weight_in,
    out_ref,
    state_ref, coef_lon_ref, coef_lat_ref, land_ref, cols_ref, count_ref, value_ref, weight_ref,
    outgoing,    recv, seen, hot, spread, spread_bf, pieces, scattered, coefs, coef_out, coef_west, coef_east,
    east_b, west_b, north_b, field, edge_out, edge_west, edge_east,
    load_sem, send_sem, recv_sem, csend_sem, crecv_sem, gsend_sem, grecv_sem,
):
    levels, rows, cols = state_ref.shape
    cells = rows * levels
    halo = PASSES
    ext = rows + 2 * halo
    lanes = cols + 128
    cap = recv.shape[3]
    lon = lax.axis_index("lon")
    lat = lax.axis_index("lat")
    east, west = lax.rem(lon + 1, n_lon), lax.rem(lon + n_lon - 1, n_lon)
    north, south = lax.rem(lat + 1, n_lat), lax.rem(lat + n_lat - 1, n_lat)

    def at(lon_to, lat_to):
        return {"lon": lon_to, "lat": lat_to}

    around = [
        at(lon, north), at(lon, south), at(east, lat), at(west, lat),
        at(east, north), at(west, north), at(east, south), at(west, south),
    ]
    loads = [
        pltpu.make_async_copy(src, dst, load_sem.at[i])
        for i, (src, dst) in enumerate((
            (value_in, value_ref), (weight_in, weight_ref), (state_in, state_ref),
            (coef_lon_in, coef_lon_ref), (coef_lat_in, coef_lat_ref), (land_in, land_ref),
            (cols_in, cols_ref), (count_in, count_ref),
        ))
    ]
    for load in loads:
        load.start()
    barrier = pltpu.get_barrier_semaphore()
    for step in range(1, n_lon):
        pl.semaphore_signal(
            barrier, inc=1, device_id=at(lax.rem(lon + step, n_lon), lat), device_id_type=MESH
        )
    for place in (0, 1, 4, 5, 6, 7):
        pl.semaphore_signal(barrier, inc=1, device_id=around[place], device_id_type=MESH)

    loads[0].wait()
    loads[1].wait()
    for peer in range(n_lon):
        outgoing[peer, 0] = value_ref[:, 0, peer * cap:(peer + 1) * cap]
        outgoing[peer, 1] = weight_ref[:, 0, peer * cap:(peer + 1) * cap]
    for load in loads[3:6]:
        load.wait()
    here = pl.ds(halo, rows)
    coefs[0, here, 0:cols] = land_ref[...].astype(F32)
    coefs[1, here, 0:cols] = coef_lon_ref[...]
    coefs[2, here, 0:cols] = coef_lat_ref[...]
    lane = lax.broadcasted_iota(jnp.int32, (rows, 128), 1)
    to_east = jnp.zeros((rows, 128), F32)
    to_west = jnp.zeros((rows, 128), F32)
    for a in range(3):
        low = coefs[a, here, 0:128]
        high = coefs[a, here, cols - 128:cols]
        mine = (lane >= 8 * a) & (lane < 8 * a + 8)
        to_east = jnp.where(mine, pltpu.roll(high, (8 * a + 8) % 128, axis=1), to_east)
        to_west = jnp.where(mine, low if a == 0 else pltpu.roll(low, 8 * a, axis=1), to_west)
    coef_out[0] = to_east
    coef_out[1] = to_west

    top, bottom = pl.ds(rows - halo, halo), pl.ds(0, halo)
    low_rim, high_rim = pl.ds(0, halo), pl.ds(halo + rows, halo)
    coef_moves = [
        (coefs.at[:, pl.ds(rows, halo), 0:cols], coefs.at[:, low_rim, 0:cols]),
        (coefs.at[:, pl.ds(halo, halo), 0:cols], coefs.at[:, high_rim, 0:cols]),
        (coef_out.at[0], coef_west.at[here]),
        (coef_out.at[1], coef_east.at[here]),
        (coef_out.at[0, top], coef_west.at[low_rim]),
        (coef_out.at[1, top], coef_east.at[low_rim]),
        (coef_out.at[0, bottom], coef_west.at[high_rim]),
        (coef_out.at[1, bottom], coef_east.at[high_rim]),
    ]
    coef_copies = [
        pltpu.make_async_remote_copy(
            src_ref=src, dst_ref=dst, send_sem=csend_sem.at[i], recv_sem=crecv_sem.at[i],
            device_id=around[i], device_id_type=MESH,
        )
        for i, (src, dst) in enumerate(coef_moves)
    ]
    pl.semaphore_wait(barrier, n_lon - 1 + 6)
    for copy in coef_copies:
        copy.start()

    def profile_copy(step):
        peer = lax.rem(lon + step, n_lon)
        return pltpu.make_async_remote_copy(
            src_ref=outgoing.at[peer],
            dst_ref=recv.at[step],
            send_sem=send_sem.at[step],
            recv_sem=recv_sem.at[step],
            device_id=at(peer, lat),
            device_id_type=MESH,
        )

    half = n_lon // 2
    order = []
    for off in range(half, 0, -1):
        order += [off] if 2 * off == n_lon else [off, n_lon - off]
    for step in order:
        profile_copy(step).start()
    recv[0] = outgoing[lon]

    for load in (loads[2], loads[6], loads[7]):
        load.wait()
    for r in range(rows):
        parts = pieces_of(state_ref[:, r, :])
        for i in range(3):
            pieces[cells * i + levels * r:cells * i + levels * (r + 1), :] = parts[i]

    def places(step):
        holder = lax.rem(lon + n_lon - step, n_lon)
        entry = cols_ref[:, pl.ds(pl.multiple_of(holder * cap, 128), cap)]
        return holder, lax.shift_right_logical(entry, cols.bit_length() - 1), entry & (cols - 1)

    def gather_step(step, carry):
        _, row, col = places(step)
        which_col = lax.broadcasted_iota(jnp.int32, (cols, cap), 0)
        one_hot = jnp.where(which_col == col, 1.0, 0.0).astype(BF16)
        hot[step] = one_hot
        spread[...] = jnp.dot(pieces[...], one_hot, preferred_element_type=F32)
        row_b = jnp.broadcast_to(row, (8, cap))
        totals = [jnp.zeros((8, cap), F32) for _ in range(0, levels, 8)]
        for r in range(rows):
            mine = row_b == r
            for h in range(levels // 8):
                at_row = pl.ds(levels * r + 8 * h, 8)
                picked = spread[at_row, :]
                for i in range(1, 3):
                    picked += spread[pl.ds(cells * i + levels * r + 8 * h, 8), :]
                totals[h] += jnp.where(mine, picked, 0.0)
        for h in range(levels // 8):
            seen[step, 8 * h:8 * h + 8] = totals[h]
        return carry

    lax.fori_loop(0, n_lon, gather_step, 0)

    for copy in coef_copies:
        copy.wait()
    lane_e = lax.broadcasted_iota(jnp.int32, (ext, 128), 1)
    from_west, from_east = coef_west[...], coef_east[...]
    for a in range(3):
        eastern = from_east if a == 0 else pltpu.roll(from_east, 128 - 8 * a, axis=1)
        western = pltpu.roll(from_west, 120 - 8 * a, axis=1)
        coefs[a, :, cols:lanes] = jnp.where(
            lane_e < 8, eastern, jnp.where(lane_e >= 120, western, 0.0)
        )
    row_place = lax.broadcasted_iota(jnp.int32, (ext, lanes), 0)
    first_out = jnp.where(lat == 0, halo, 0)
    last_out = jnp.where(lat == n_lat - 1, halo + rows, ext)
    inside = (row_place >= first_out) & (row_place < last_out)
    sea = jnp.where(inside, coefs[0], 0.0)
    coefs[0] = sea
    east_face = coefs[1] * sea * pltpu.roll(sea, lanes - 1, axis=1)
    north_face = coefs[2] * sea * pltpu.roll(sea, ext - 1, axis=0)
    west_face = pltpu.roll(east_face, 1, axis=1)
    for e in range(ext):
        west_b[e] = jnp.broadcast_to(west_face[e:e + 1, :], (8, lanes))
        east_b[e] = jnp.broadcast_to(east_face[e:e + 1, :], (8, lanes))
        north_b[e] = jnp.broadcast_to(north_face[e:e + 1, :], (8, lanes))

    scattered[...] = jnp.zeros_like(scattered)

    def scatter_step(turn, carry):
        off = half - turn // 2
        step = jnp.where(turn == 0, 0, jnp.where(turn % 2 == 1, n_lon - off, off))
        holder, row, _ = places(step)

        @pl.when(step != 0)
        def _():
            profile_copy(step).wait_recv()

        slot = lax.broadcasted_iota(jnp.int32, (levels, cap), 1)
        usable = jnp.where(slot < count_ref[0, holder], 1.0, 0.0)
        weighted = recv[step, 1] * (recv[step, 0] - seen[step]) * usable
        parts = pieces_of(weighted)[:2]
        row_b = jnp.broadcast_to(row.astype(F32), (levels, cap)).astype(BF16)
        nothing = jnp.zeros((levels, cap), BF16)
        for r in range(rows):
            mine = row_b == jnp.asarray(r, BF16)
            for i in range(2):
                start = cells * i + levels * r
                spread_bf[start:start + levels, :] = jnp.where(mine, parts[i], nothing)
        total = lax.dot_general(
            spread_bf[...], hot[step], (((1,), (1,)), ((), ())), preferred_element_type=F32
        )
        scattered[...] += total[:cells] + total[cells:]
        return carry

    lax.fori_loop(0, n_lon, scatter_step, 0)

    group = 128 // halo
    blocks = rows // group
    middle = pl.ds(1, blocks)
    field_moves = [
        (field.at[0, pl.ds(rows, halo), :, 0:cols], field.at[0, low_rim, :, 0:cols]),
        (field.at[0, pl.ds(halo, halo), :, 0:cols], field.at[0, high_rim, :, 0:cols]),
        (edge_out.at[0], edge_west.at[middle]),
        (edge_out.at[1], edge_east.at[middle]),
        (edge_out.at[0, blocks - 1], edge_west.at[0]),
        (edge_out.at[1, blocks - 1], edge_east.at[0]),
        (edge_out.at[0, 0], edge_west.at[blocks + 1]),
        (edge_out.at[1, 0], edge_east.at[blocks + 1]),
    ]
    field_copies = [
        pltpu.make_async_remote_copy(
            src_ref=src, dst_ref=dst, send_sem=gsend_sem.at[i], recv_sem=grecv_sem.at[i],
            device_id=around[i], device_id_type=MESH,
        )
        for i, (src, dst) in enumerate(field_moves)
    ]
    border = list(range(halo)) + list(range(rows - halo, rows))
    for r in border + list(range(halo, rows - halo)):
        if r == halo:
            field_copies[0].start()
            field_copies[1].start()
        sea_r = jnp.broadcast_to(coefs[0, halo + r:halo + r + 1, 0:cols], (levels, cols))
        field[0, halo + r, :, 0:cols] = scattered[levels * r:levels * (r + 1), :] * sea_r
    lane_g = lax.broadcasted_iota(jnp.int32, (levels, 128), 1)
    for j in range(blocks):
        to_east = jnp.zeros((levels, 128), F32)
        to_west = jnp.zeros((levels, 128), F32)
        for k in range(group):
            low = field[0, halo + j * group + k, :, 0:128]
            high = field[0, halo + j * group + k, :, cols - 128:cols]
            mine = (lane_g >= 8 * k) & (lane_g < 8 * k + 8)
            to_east = jnp.where(mine, pltpu.roll(high, (8 * k + 8) % 128, axis=1) if k < group - 1 else high, to_east)
            to_west = jnp.where(mine, low if k == 0 else pltpu.roll(low, 8 * k, axis=1), to_west)
        edge_out[0, j] = to_east
        edge_out[1, j] = to_west
    for i in range(2, 8):
        field_copies[i].start()

    def unpack(first, last):
        for e in range(first, last):
            j, k = (e + halo) // group, (e + halo) % group
            eastern = edge_east[j]
            if k > 0:
                eastern = pltpu.roll(eastern, 128 - 8 * k, axis=1)
            western = edge_west[j]
            if k < group - 1:
                western = pltpu.roll(western, 120 - 8 * k, axis=1)
            field[0, e, :, cols:lanes] = jnp.where(
                lane_g < 8, eastern, jnp.where(lane_g >= 120, western, 0.0)
            )

    def twice(face):
        return jnp.concatenate([face] * (levels // 8), axis=0)

    def advance(t, first, last):
        g = field[t - 1, first]
        flux_south = twice(north_b[first - 1]) * (g - field[t - 1, first - 1])
        for e in range(first, last):
            g_north = field[t - 1, e + 1]
            flux_north = twice(north_b[e]) * (g_north - g)
            flux_east = twice(east_b[e]) * (pltpu.roll(g, lanes - 1, axis=1) - g)
            flux_west = twice(west_b[e]) * (g - pltpu.roll(g, 1, axis=1))
            new = g + flux_east - flux_west + flux_north - flux_south
            if t == PASSES:
                out_ref[:, e - halo, :] = new[:, 0:cols]
            else:
                field[t, e] = new
            g, flux_south = g_north, flux_north

    field_copies[2].wait_recv()
    field_copies[3].wait_recv()
    unpack(halo, halo + rows)
    for t in range(1, PASSES + 1):
        advance(t, halo + t, halo + rows - t)
    for i in (0, 1, 4, 5, 6, 7):
        field_copies[i].wait_recv()
    unpack(0, halo)
    unpack(halo + rows, ext)
    for t in range(1, PASSES + 1):
        advance(t, t, halo + t)
        advance(t, halo + rows - t, ext - t)

    for step in order:
        profile_copy(step).wait_send()
    for copy in field_copies:
        copy.wait_send()


def body(state, coef_lon, coef_lat, land_sea, send_cols, send_count, obs_value, obs_weight):
    levels, rows, cols = state.shape
    n_lon = lax.axis_size("lon")
    n_lat = lax.axis_size("lat")
    slots = send_cols.shape[1]
    cap = slots // n_lon
    ext, lanes = rows + 2 * PASSES, cols + 128
    blocks = rows * PASSES // 128
    vmem = pl.BlockSpec(memory_space=pltpu.VMEM)
    dma = pltpu.SemaphoreType.DMA
    return pl.pallas_call(
        functools.partial(kernel, n_lon, n_lat),
        out_shape=jax.ShapeDtypeStruct((levels, rows, cols), F32),
        in_specs=[pl.BlockSpec(memory_space=pltpu.HBM)] * 8,
        out_specs=vmem,
        scratch_shapes=[
            pltpu.VMEM((levels, rows, cols), F32),
            pltpu.VMEM((rows, cols), F32),
            pltpu.VMEM((rows, cols), F32),
            pltpu.VMEM((rows, cols), jnp.int32),
            pltpu.VMEM((1, slots), jnp.int32),
            pltpu.SMEM((1, n_lon), jnp.int32),
            pltpu.VMEM((levels, 1, slots), F32),
            pltpu.VMEM((levels, 1, slots), F32),
            pltpu.VMEM((n_lon, 2, levels, cap), F32),
            pltpu.VMEM((n_lon, 2, levels, cap), F32),
            pltpu.VMEM((n_lon, levels, cap), F32),
            pltpu.VMEM((n_lon, cols, cap), BF16),
            pltpu.VMEM((3 * rows * levels, cap), F32),
            pltpu.VMEM((2 * rows * levels, cap), BF16),
            pltpu.VMEM((3 * rows * levels, cols), BF16),
            pltpu.VMEM((rows * levels, cols), F32),
            pltpu.VMEM((3, ext, lanes), F32),
            pltpu.VMEM((2, rows, 128), F32),
            pltpu.VMEM((ext, 128), F32),
            pltpu.VMEM((ext, 128), F32),
            pltpu.VMEM((ext, 8, lanes), F32),
            pltpu.VMEM((ext, 8, lanes), F32),
            pltpu.VMEM((ext, 8, lanes), F32),
            pltpu.VMEM((PASSES, ext, levels, lanes), F32),
            pltpu.VMEM((2, blocks, levels, 128), F32),
            pltpu.VMEM((blocks + 2, levels, 128), F32),
            pltpu.VMEM((blocks + 2, levels, 128), F32),
            dma((8,)),
            dma((n_lon,)),
            dma((n_lon,)),
            dma((8,)),
            dma((8,)),
            dma((8,)),
            dma((8,)),
        ],
        compiler_params=pltpu.CompilerParams(
            collective_id=0, has_side_effects=True, vmem_limit_bytes=64 * 2**20
        ),
        name="analysis",
    )(
        state, coef_lon, coef_lat, land_sea, send_cols, send_count,
        obs_value, obs_weight,
    )


def solution(mesh):
    placed = (
        P(None, "lat", "lon"),
        P("lat", "lon"),
        P("lat", "lon"),
        P("lat", "lon"),
        P("lat", "lon"),
        P("lat", "lon"),
        P(None, "lat", "lon"),
        P(None, "lat", "lon"),
    )
    return jax.shard_map(
        body, mesh=mesh, in_specs=placed, out_specs=P(None, "lat", "lon"), check_vma=False
    )
```
